32 devices in a mesh: fac: 8 (over z, y), scn: 4 (over x, core).
Axes of the slice: x: 2, y: 2, z: 4, core: 2. Of those that a mesh axis runs over, the one named last changes fastest.
Arguments:
- loadings: bfloat16 [49152, 512], P('fac'), may hold values from -0.25 to 0.25
- draws: bfloat16 [512, 3072], P(None, 'scn'), may hold values from -6 to 6
- delta: float32 [49152], P('fac'), may hold values from -0.02734375 to 0.02734375
- gamma: bfloat16 [128, 128, 128], P('fac', 'scn'), may hold values from -0.0029296875 to 0.0029296875
- pair_rows: int32 [128], replicated, may hold values from 0 to 383, as said below
- pair_cols: int32 [128], replicated, may hold values from 0 to 383, as said below
- pair_count: int32 [8], replicated, may hold values from 4 to 16, as said below
Outputs:
- pnl: float32 [3072], P('scn')
The draws below stay inside these ranges and needn't reach their ends.
Inputs may be any that keep to these rules, and one draw needn't show every extreme that they name: Block numbers of the slots; for every owner o, among the 32 entries pair_rows and pair_cols of its slots (live or not), the blocks of each index h of fac (blocks h * 48 to h * 48 + 47) are named at most 5 times, and for every owner some index h is named exactly 5 times. `pair_cols`: see pair_rows; the bound holds with both lists together. An owner's live slots are its first pair_count slots; some owner has all 16 slots live.
All inputs are finite; a program needn't handle non-finite values.
Results may differ from the reference program's by a relative error of at most 0.002.
Values may be sent and summed in bfloat16 or wider, within the bound.
A program may use at most 128 MiB of HBM per device.

```python
import jax
import jax.numpy as jnp
from jax import lax

BLK = 128
BLK_DEV = 48
K = 512
S_DEV = 768
CAP = 16
FACTORS = 49152
BLOCKS = 384
PAIRS = 128
MOST = 5
SCEN = 3072
N_SCN = 4


def owner_table(owner_key):
    holders = BLOCKS // BLK_DEV
    entries = 2 * CAP
    base = MOST - 1
    index = jnp.arange(entries, dtype=jnp.int32)
    chosen = jax.random.permutation(jax.random.fold_in(owner_key, 1), holders).astype(jnp.int32)
    heavy = chosen[0]
    doubled = chosen[1]
    first_donor = chosen[2]
    second_donor = chosen[3]
    listing = index // base
    listing = jnp.where(index == first_donor * base, heavy, listing).astype(jnp.int32)
    listing = jnp.where(index == second_donor * base, doubled, listing).astype(jnp.int32)
    pulled = (index == doubled * base) | (index == second_donor * base)
    order = jnp.argsort(jnp.where(pulled, 0, 1).astype(jnp.int32), stable=True)
    remaining = listing[order][2:]
    remaining = jax.random.permutation(jax.random.fold_in(owner_key, 3), remaining)
    diag_slot = jax.random.randint(jax.random.fold_in(owner_key, 4), (), 0, CAP // 4).astype(jnp.int32)
    slot_of = index // 2
    shifted = jnp.where(index > 2 * diag_slot + 1, index - 2, index)
    shifted = jnp.clip(shifted, 0, entries - 3)
    holder = jnp.where(slot_of == diag_slot, doubled, remaining[shifted]).astype(jnp.int32)
    same_holder = holder[:, None] == holder[None, :]
    earlier = index[None, :] < index[:, None]
    within_rank = jnp.sum((same_holder & earlier).astype(jnp.int32), axis=1).astype(jnp.int32)
    holder_start = jax.random.randint(jax.random.fold_in(owner_key, 5), (holders,), 0, BLK_DEV).astype(jnp.int32)
    offset = ((holder_start[holder] + within_rank) % BLK_DEV).astype(jnp.int32)
    paired_offset = offset.reshape(CAP, 2)
    col_offset = jnp.where(jnp.arange(CAP, dtype=jnp.int32) == diag_slot, paired_offset[:, 0], paired_offset[:, 1])
    offset = jnp.stack([paired_offset[:, 0], col_offset], axis=1).reshape(-1)
    return (holder * BLK_DEV + offset).astype(jnp.int32)


def request_table(key):
    owners = PAIRS // CAP
    base = jax.random.fold_in(key, 11)
    owner_keys = jax.random.split(jax.random.fold_in(base, 1), owners)
    return jax.vmap(owner_table)(owner_keys)


def draw_pair_rows(key, part):
    return request_table(key)[:, 0::2].reshape(-1)


def draw_pair_cols(key, part):
    return request_table(key)[:, 1::2].reshape(-1)


def draw_pair_count(key, part):
    owners = PAIRS // CAP
    counts = jax.random.randint(jax.random.fold_in(key, 21), (owners,), CAP // 4, 3 * CAP // 4 + 1)
    picked = jax.random.randint(jax.random.fold_in(key, 22), (), 0, owners)
    return jnp.where(jnp.arange(owners) == picked, CAP, counts).astype(jnp.int32)


def block_levels(key, dims, cuts, smallest, top_value):
    level, own = 1.0, jax.random.fold_in(key, 6)
    for position, shards_of in cuts:
        heights = jnp.exp(jax.random.uniform(jax.random.fold_in(own, position), (shards_of,), jnp.float32, smallest / len(cuts), top_value / len(cuts)))
        level = level * jnp.repeat(heights, dims[position] // shards_of).reshape([-1 if axis == position else 1 for axis in range(len(dims))])
    return level


def normal_values(rng, shape, deviation, most, pieces=(), kind=jnp.bfloat16):
    values = jax.random.normal(rng, shape, jnp.float32) * deviation
    if len(pieces) > 0:
        values = block_levels(rng, shape, pieces, -0.22, 0.18) * values
    return jnp.clip(values, min=-most, max=most).astype(kind)


def setup_inputs(seed: int = 0) -> dict:
    streams_of = jax.random.split(jax.random.key(seed), 8)
    return {
        "loadings": normal_values(streams_of[0], (FACTORS, K), K ** -0.5, 0.25, ((0, 8),)),
        "draws": normal_values(streams_of[1], (K, SCEN), 1.0, 6.0, ((1, 4),)),
        "delta": normal_values(streams_of[2], (FACTORS,), FACTORS ** -0.5, 0.02734375, ((0, 8),), jnp.float32),
        "gamma": normal_values(streams_of[3], (PAIRS, BLK, BLK), (BLK * BLK * PAIRS * 2) ** -0.5, 0.0029296875, ((0, 8), (1, 4))),
        "pair_rows": draw_pair_rows(jax.random.fold_in(streams_of[7], 71), 0),
        "pair_cols": draw_pair_cols(jax.random.fold_in(streams_of[7], 71), 0),
        "pair_count": draw_pair_count(jax.random.fold_in(streams_of[7], 71), 0),
    }


def reference(loadings, draws, delta, gamma, pair_rows, pair_cols, pair_count):
    owners = PAIRS // CAP
    blocks = loadings.shape[0] // BLK
    is_live = jnp.arange(CAP, dtype=jnp.int32)[None, :] < pair_count[:, None]
    weight = jnp.where(pair_rows == pair_cols, 1.0, 2.0).astype(jnp.float32) * is_live.reshape(-1).astype(jnp.float32)
    gamma_owned = gamma.reshape(owners, CAP, BLK, BLK)
    rows_owned = pair_rows.reshape(owners, CAP)
    cols_owned = pair_cols.reshape(owners, CAP)
    weight_owned = weight.reshape(owners, CAP)

    def one_group(draw_block):
        exposure = jnp.dot(loadings, draw_block, preferred_element_type=jnp.float32)
        linear = jnp.sum(delta[:, None] * exposure, axis=0)
        shocks = exposure.astype(jnp.bfloat16).reshape(blocks, BLK, S_DEV)

        def per_owner(items):
            gamma_block, row_ids, col_ids, slot_weight = items
            left_block = shocks[row_ids].astype(jnp.float32)
            right_block = shocks[col_ids].astype(jnp.float32)
            product = jnp.einsum("cab,cbs->cas", gamma_block.astype(jnp.float32), right_block)
            return jnp.sum(slot_weight[:, None] * jnp.sum(product * left_block, axis=1), axis=0)

        parts = lax.map(per_owner, (gamma_owned, rows_owned, cols_owned, weight_owned))
        return linear + 0.5 * jnp.sum(parts, axis=0)

    groups = draws.reshape(K, N_SCN, S_DEV).transpose(1, 0, 2)
    return lax.map(one_group, groups).reshape(-1)
```

```python
import functools

import jax
import jax.numpy as jnp
from jax import lax
from jax.experimental import pallas as pl
from jax.experimental.pallas import tpu as pltpu
from jax.sharding import PartitionSpec as P

MESH = pl.DeviceIdType.MESH
CHUNKS = 8


def pack(owners, per_source, capacity, part,
         rows_ref, cols_ref, count_ref, load_ref,
         out_ref, own_ref, arrival_ref, weight_ref, index, seen, sems, own_sems):
    me = lax.axis_index("fac")
    mine = lax.axis_index("scn")
    local_blocks = load_ref.shape[0]
    low = me * local_blocks
    strip = pl.ds(pl.multiple_of(mine * part, part), part)

    def one_owner(step, carry):
        owner = lax.rem(me + step, owners)
        base = owner * capacity
        count = jnp.int32(0)
        for request in range(2 * capacity):
            ref = rows_ref if request % 2 == 0 else cols_ref
            offset = ref[base + request // 2] - low
            index[count] = offset
            count = count + ((offset >= 0) & (offset < local_blocks)).astype(jnp.int32)
        for k in range(per_source):
            block = jnp.where(k < count, index[k], 0)

            @pl.when(step > 0)
            def _():
                pltpu.make_async_copy(
                    load_ref.at[block, strip, :], out_ref.at[owner, k], sems.at[step, k]
                ).start()

            @pl.when(step == 0)
            def _():
                pltpu.make_async_copy(load_ref.at[block], own_ref.at[k], own_sems.at[k]).start()

        return carry

    for k in range(per_source + 1):
        index[k] = 0
    lax.fori_loop(1, owners, one_owner, 0)
    one_owner(0, 0)

    for h in range(owners):
        seen[h] = 0
    base = me * capacity
    for request in range(2 * capacity):
        ref = rows_ref if request % 2 == 0 else cols_ref
        source = lax.div(ref[base + request // 2], jnp.int32(local_blocks))
        position = seen[source]
        arrival_ref[request] = source * per_source + position
        seen[source] = position + 1
    live = count_ref[me]
    for slot in range(capacity):
        level = jnp.where(rows_ref[base + slot] == cols_ref[base + slot], 0.5, 1.0)
        weight_ref[slot] = jnp.where(slot < live, level, 0.0).astype(jnp.float32)

    def finish(step, carry):
        for k in range(per_source):
            pltpu.make_async_copy(
                load_ref.at[0, strip, :], out_ref.at[lax.rem(me + step, owners), k], sems.at[step, k]
            ).wait()
        return carry

    lax.fori_loop(1, owners, finish, 0)
    for k in range(per_source):
        pltpu.make_async_copy(load_ref.at[0], own_ref.at[k], own_sems.at[k]).wait()


def three_parts(values):
    first = values.astype(jnp.bfloat16).astype(jnp.float32)
    rest = values - first
    second = rest.astype(jnp.bfloat16).astype(jnp.float32)
    third = rest - second
    shape = (16, values.shape[1])
    row = lax.broadcasted_iota(jnp.int32, shape, 0)
    spread = [jnp.broadcast_to(v, shape) for v in (first, second, third)]
    zero = jnp.zeros(shape, jnp.float32)
    both = jnp.where(row == 0, spread[0], jnp.where(row == 1, spread[1], jnp.where(row == 2, spread[2], zero)))
    return both.astype(jnp.bfloat16)


def main_kernel(owners, groups, per_source, capacity, part,
                arrival_ref, weight_ref, out_q, own_hbm, load_hbm, draws_hbm, delta_ref, gamma_hbm,
                result_ref,
                loads, draws, own, inbound, shocks, gam, fold, linear, sums,
                load_sem, in_sem, main_s, main_r, x_s, x_r, core_s, core_r, sum_s, sum_r):
    me = lax.axis_index("fac")
    mine = lax.axis_index("scn")
    chips = groups // 2
    core = lax.rem(mine, 2)
    chip = lax.div(mine, 2)
    partner = mine + 1 - 2 * core

    def wrap(value, size):
        return lax.rem(value + size, size)

    def group_of(chip_index):
        return chip_index * 2 + core

    def strip(q):
        return pl.ds(pl.multiple_of(q * part, part), part)

    barrier = pltpu.get_barrier_semaphore()
    for d in range(1, owners):
        pl.semaphore_signal(barrier, inc=1, device_id={"fac": wrap(me + d, owners)}, device_id_type=MESH)
    for j in range(1, chips):
        pl.semaphore_signal(barrier, inc=1, device_id={"scn": group_of(wrap(chip + j, chips))}, device_id_type=MESH)
    pl.semaphore_signal(barrier, inc=1, device_id={"scn": partner}, device_id_type=MESH)

    gamma_in = pltpu.make_async_copy(gamma_hbm, gam.at[:, strip(mine), :], in_sem.at[0])
    draws_in = pltpu.make_async_copy(draws_hbm, draws, in_sem.at[1])
    own_in = pltpu.make_async_copy(own_hbm, own, in_sem.at[2])
    gamma_in.start()
    draws_in.start()
    own_in.start()
    rows = loads.shape[1]

    def load_copy(c):
        return pltpu.make_async_copy(
            load_hbm.at[pl.ds(pl.multiple_of(c * rows, rows), rows), :], loads.at[c], load_sem.at[c]
        )

    for c in range(CHUNKS):
        load_copy(c).start()

    pl.semaphore_wait(barrier, owners - 1 + chips)

    def main_copy(d):
        return pltpu.make_async_remote_copy(
            src_ref=out_q.at[wrap(me + d, owners)], dst_ref=inbound.at[me, :, strip(mine), :],
            send_sem=main_s.at[d], recv_sem=main_r.at[d],
            device_id={"fac": wrap(me + d, owners)}, device_id_type=MESH,
        )

    def main_arrival(d):
        return pltpu.make_async_remote_copy(
            src_ref=out_q.at[me], dst_ref=inbound.at[wrap(me - d, owners), :, strip(mine), :],
            send_sem=main_s.at[d], recv_sem=main_r.at[d],
            device_id={"fac": wrap(me + d, owners)}, device_id_type=MESH,
        )

    def start_main(d, carry):
        main_copy(d).start()
        return carry

    lax.fori_loop(1, owners, start_main, 0)

    def place(d, q):
        if d is None:
            return gam.at[:, strip(q), :]
        return inbound.at[wrap(me - d, owners), :, strip(q), :]

    def at(d):
        return 0 if d is None else d

    def x_copy(d, j, q, source=None):
        return pltpu.make_async_remote_copy(
            src_ref=place(d, q) if source is None else source, dst_ref=place(d, q),
            send_sem=x_s.at[at(d), j - 1], recv_sem=x_r.at[at(d), j - 1],
            device_id={"scn": group_of(wrap(chip + j, chips))}, device_id_type=MESH,
        )

    def core_copy(d, j, q, source=None):
        return pltpu.make_async_remote_copy(
            src_ref=place(d, q) if source is None else source, dst_ref=place(d, q),
            send_sem=core_s.at[at(d), j], recv_sem=core_r.at[at(d), j],
            device_id={"scn": partner}, device_id_type=MESH,
        )

    def origin(j):
        return group_of(wrap(chip - j, chips))

    def partners_origin(j):
        return wrap(chip - j, chips) * 2 + 1 - core

    def share(d, source=None):
        for j in range(1, chips):
            x_copy(d, j, mine, source).start()
        core_copy(d, 0, mine, source).start()

    def forward(d):
        for j in range(1, chips):
            x_copy(d, j, origin(j)).wait_recv()
            core_copy(d, j, origin(j)).start()

    def gathered(d):
        for j in range(chips):
            core_copy(d, j, partners_origin(j)).wait_recv()

    def drain(d):
        for j in range(1, chips):
            x_copy(d, j, mine).wait_send()
        core_copy(d, 0, mine).wait_send()
        for j in range(1, chips):
            core_copy(d, j, origin(j)).wait_send()

    share(None, gamma_hbm)
    draws_in.wait()
    own_in.wait()

    def expose(blocks, h):
        flat = blocks.reshape(blocks.shape[0] * blocks.shape[1], blocks.shape[2])
        value = jnp.dot(flat, draws[...], preferred_element_type=jnp.float32).astype(jnp.bfloat16)
        shocks[pl.ds(h * per_source, per_source)] = value.reshape(per_source, blocks.shape[1], value.shape[1])

    expose(own[...], me)
    fold[...] = jnp.zeros_like(fold)

    def step(t, carry):
        @pl.when(t < owners)
        def _():
            main_arrival(t).wait_recv()
            share(t)

        @pl.when(t == 1)
        def _():
            forward(None)

        @pl.when((t > 1) & (t <= owners))
        def _():
            forward(t - 1)

        @pl.when(t <= CHUNKS)
        def _():
            load_copy(t - 1).wait()
            piece = delta_ref[:, pl.ds(pl.multiple_of((t - 1) * rows, rows), rows)]
            fold[...] += jnp.dot(three_parts(piece), loads[t - 1], preferred_element_type=jnp.float32)

        @pl.when(t == owners)
        def _():
            total = jnp.sum(fold[...], axis=0, keepdims=True)
            linear[...] = jnp.dot(three_parts(total), draws[...], preferred_element_type=jnp.float32)

        @pl.when(t > 2)
        def _():
            gathered(t - 2)
            h = wrap(me - (t - 2), owners)
            expose(inbound[h], h)

        return carry

    lax.fori_loop(1, owners + 2, step, 0)
    gamma_in.wait()
    gathered(None)

    columns = draws.shape[1]
    height = gam.shape[1]

    def one_slot(p, total):
        product = jnp.dot(gam[p], shocks[arrival_ref[2 * p + 1]], preferred_element_type=jnp.float32)
        terms = product * shocks[arrival_ref[2 * p]].astype(jnp.float32)
        return total + weight_ref[p] * jnp.sum(terms.reshape(height // 8, 8, columns), axis=0)

    quad = lax.fori_loop(0, capacity, one_slot, jnp.zeros((8, columns), jnp.float32))
    part_sum = jnp.sum(quad, axis=0, keepdims=True) + jnp.sum(linear[...], axis=0, keepdims=True)
    sums[me] = part_sum

    def sum_copy(d):
        return pltpu.make_async_remote_copy(
            src_ref=sums.at[me], dst_ref=sums.at[me],
            send_sem=sum_s.at[d], recv_sem=sum_r.at[d],
            device_id={"fac": wrap(me + d, owners)}, device_id_type=MESH,
        )

    def sum_arrival(d):
        return pltpu.make_async_remote_copy(
            src_ref=sums.at[wrap(me - d, owners)], dst_ref=sums.at[wrap(me - d, owners)],
            send_sem=sum_s.at[d], recv_sem=sum_r.at[d],
            device_id={"fac": wrap(me + d, owners)}, device_id_type=MESH,
        )

    def start_sum(d, carry):
        sum_copy(d).start()
        return carry

    lax.fori_loop(1, owners, start_sum, 0)
    drain(None)

    def drain_step(d, carry):
        main_copy(d).wait_send()
        drain(d)
        return carry

    lax.fori_loop(1, owners, drain_step, 0)

    def wait_sum(d, carry):
        sum_arrival(d).wait_recv()
        return carry

    lax.fori_loop(1, owners, wait_sum, 0)
    result_ref[...] = jnp.sum(sums[...], axis=0)

    def drain_sum(d, carry):
        sum_copy(d).wait_send()
        return carry

    lax.fori_loop(1, owners, drain_sum, 0)


def on_device(loadings, draws, delta, gamma, pair_rows, pair_cols, pair_count):
    owners = lax.axis_size("fac")
    groups = lax.axis_size("scn")
    capacity, part, height = gamma.shape
    local_blocks = loadings.shape[0] // height
    depth, columns = draws.shape
    per_source = 2 * capacity // owners + 1
    chips = groups // 2
    smem = pl.BlockSpec(memory_space=pltpu.SMEM)
    anywhere = pl.BlockSpec(memory_space=pl.ANY)
    vmem = pl.BlockSpec(memory_space=pltpu.VMEM)
    bf16, f32, i32 = jnp.bfloat16, jnp.float32, jnp.int32
    dma = pltpu.SemaphoreType.DMA

    outbound, own, arrival, weight = pl.pallas_call(
        functools.partial(pack, owners, per_source, capacity, part),
        out_shape=(
            jax.ShapeDtypeStruct((owners, per_source, part, depth), bf16),
            jax.ShapeDtypeStruct((per_source, height, depth), bf16),
            jax.ShapeDtypeStruct((2 * capacity,), i32),
            jax.ShapeDtypeStruct((capacity,), f32),
        ),
        in_specs=[smem, smem, smem, anywhere],
        out_specs=(anywhere, anywhere, smem, smem),
        scratch_shapes=[
            pltpu.SMEM((2 * capacity + 1,), i32),
            pltpu.SMEM((owners,), i32),
            dma((owners, per_source)),
            dma((per_source,)),
        ],
        name="pack",
    )(pair_rows, pair_cols, pair_count, loadings.reshape(local_blocks, height, depth))

    rows = loadings.shape[0] // CHUNKS
    result = pl.pallas_call(
        functools.partial(main_kernel, owners, groups, per_source, capacity, part),
        out_shape=jax.ShapeDtypeStruct((1, columns), f32),
        in_specs=[smem, smem, anywhere, anywhere, anywhere, anywhere, vmem, anywhere],
        out_specs=vmem,
        scratch_shapes=[
            pltpu.VMEM((CHUNKS, rows, depth), bf16),
            pltpu.VMEM((depth, columns), bf16),
            pltpu.VMEM((per_source, height, depth), bf16),
            pltpu.VMEM((owners, per_source, height, depth), bf16),
            pltpu.VMEM((owners * per_source, height, columns), bf16),
            pltpu.VMEM((capacity, height, height), bf16),
            pltpu.VMEM((16, depth), f32),
            pltpu.VMEM((16, columns), f32),
            pltpu.VMEM((owners, 1, columns), f32),
            dma((CHUNKS,)),
            dma((3,)),
            dma((owners,)),
            dma((owners,)),
            dma((owners, max(chips - 1, 1))),
            dma((owners, max(chips - 1, 1))),
            dma((owners, chips)),
            dma((owners, chips)),
            dma((owners,)),
            dma((owners,)),
        ],
        compiler_params=pltpu.CompilerParams(
            collective_id=0, has_side_effects=True, vmem_limit_bytes=52 * 2**20
        ),
        name="gather_and_sum",
    )(arrival, weight, outbound, own, loadings, draws, delta.reshape(1, -1), gamma)
    return result.reshape(columns)


def solution(mesh):
    in_specs = (P("fac", None), P(None, "scn"), P("fac"), P("fac", "scn", None), P(), P(), P())
    out_specs = P("scn")
    return jax.shard_map(
        on_device, mesh=mesh, in_specs=in_specs, out_specs=out_specs, check_vma=False
    )
```

```python
import functools

import jax
import jax.numpy as jnp
from jax import lax
from jax.experimental import pallas as pl
from jax.experimental.pallas import tpu as pltpu
from jax.sharding import PartitionSpec as P

MESH = pl.DeviceIdType.MESH
CHUNKS = 8


def tabulate(owners, per_source, local_blocks, wanted_ref, count_ref, table_ref):
    me = lax.axis_index("fac")
    wanted = wanted_ref[...]
    requests = wanted.shape[1]
    capacity = requests // 2
    f32, i32 = jnp.float32, jnp.int32
    holder = ((wanted.astype(f32) + 0.5) * (1.0 / local_blocks)).astype(i32)
    square = (requests, requests)
    earlier = (
        lax.broadcasted_iota(i32, square, 0) < lax.broadcasted_iota(i32, square, 1)
    ).astype(f32)

    def rank_of(hit):
        return jnp.dot(hit.astype(f32), earlier, preferred_element_type=f32).astype(i32)

    hit = holder == me
    rank = rank_of(hit)
    offset = wanted - me * local_blocks
    lane = lax.broadcasted_iota(i32, (owners, 128), 1)
    picks = jnp.zeros((owners, 128), i32)
    for k in range(per_source):
        pick = jnp.sum(jnp.where(hit & (rank == k), offset, 0), axis=1, keepdims=True)
        picks = picks + jnp.where(lane == k, pick, 0)
    table_ref[0:owners] = picks

    owner = lax.broadcasted_iota(i32, wanted.shape, 0)
    is_mine = owner == me
    my_wanted = jnp.sum(jnp.where(is_mine, wanted, 0), axis=0, keepdims=True)
    my_holder = jnp.sum(jnp.where(is_mine, holder, 0), axis=0, keepdims=True)
    from_holder = owner == my_holder
    position = jnp.sum(jnp.where(from_holder, rank_of(from_holder), 0), axis=0, keepdims=True)
    arrival = my_holder * per_source + position
    slot = lax.broadcasted_iota(i32, (1, capacity), 1)
    level = jnp.where(my_wanted[:, :capacity] == my_wanted[:, capacity:], 1, 2)
    level = jnp.where(slot < count_ref[me], level, 0)
    table_ref[owners:owners + 1, 0:requests] = arrival
    table_ref[owners + 1:owners + 2, 0:capacity] = level


def three_parts(values):
    first = values.astype(jnp.bfloat16).astype(jnp.float32)
    rest = values - first
    second = rest.astype(jnp.bfloat16).astype(jnp.float32)
    third = rest - second
    shape = (16, values.shape[1])
    row = lax.broadcasted_iota(jnp.int32, shape, 0)
    spread = [jnp.broadcast_to(v, shape) for v in (first, second, third)]
    zero = jnp.zeros(shape, jnp.float32)
    both = jnp.where(row == 0, spread[0], jnp.where(row == 1, spread[1], jnp.where(row == 2, spread[2], zero)))
    return both.astype(jnp.bfloat16)


def main_kernel(owners, groups, per_source, capacity, part,
                table_ref, load_hbm, draws_hbm, delta_ref, gamma_hbm,
                result_ref,
                loads, draws, strips, out_q, inbound, shocks, gam, fold, linear, sums,
                load_sem, in_sem, main_s, main_r, x_s, x_r, core_s, core_r, sum_s, sum_r):
    me = lax.axis_index("fac")
    mine = lax.axis_index("scn")
    chips = groups // 2
    core = lax.rem(mine, 2)
    chip = lax.div(mine, 2)
    partner = mine + 1 - 2 * core

    def wrap(value, size):
        return lax.rem(value + size, size)

    def group_of(chip_index):
        return chip_index * 2 + core

    def strip(q):
        return pl.ds(pl.multiple_of(q * part, part), part)

    barrier = pltpu.get_barrier_semaphore()
    for d in range(1, owners):
        pl.semaphore_signal(barrier, inc=1, device_id={"fac": wrap(me + d, owners)}, device_id_type=MESH)
    for j in range(1, chips):
        pl.semaphore_signal(barrier, inc=1, device_id={"scn": group_of(wrap(chip + j, chips))}, device_id_type=MESH)
    pl.semaphore_signal(barrier, inc=1, device_id={"scn": partner}, device_id_type=MESH)

    gamma_in = pltpu.make_async_copy(gamma_hbm, gam.at[:, strip(mine), :], in_sem.at[0])
    draws_in = pltpu.make_async_copy(draws_hbm, draws, in_sem.at[1])
    strips_in = pltpu.make_async_copy(load_hbm.at[:, strip(mine), :], strips, in_sem.at[2])
    strips_in.start()
    gamma_in.start()
    draws_in.start()
    local_blocks, height, depth = loads.shape
    some = local_blocks // CHUNKS
    rows = some * height

    def load_copy(c):
        return pltpu.make_async_copy(
            load_hbm.at[pl.ds(c * some, some)], loads.at[pl.ds(c * some, some)], load_sem.at[c]
        )

    for c in range(CHUNKS):
        load_copy(c).start()

    pl.semaphore_wait(barrier, owners - 1 + chips)

    def main_copy(d):
        return pltpu.make_async_remote_copy(
            src_ref=out_q.at[wrap(me + d, owners)], dst_ref=inbound.at[me, :, strip(mine), :],
            send_sem=main_s.at[d], recv_sem=main_r.at[d],
            device_id={"fac": wrap(me + d, owners)}, device_id_type=MESH,
        )

    def main_arrival(d):
        return pltpu.make_async_remote_copy(
            src_ref=out_q.at[me], dst_ref=inbound.at[wrap(me - d, owners), :, strip(mine), :],
            send_sem=main_s.at[d], recv_sem=main_r.at[d],
            device_id={"fac": wrap(me + d, owners)}, device_id_type=MESH,
        )

    strips_in.wait()

    def start_main(d, carry):
        owner = wrap(me + d, owners)
        for k in range(per_source):
            out_q[owner, k] = strips[table_ref[owner, k]]
        main_copy(d).start()
        return carry

    lax.fori_loop(1, owners, start_main, 0)

    def place(d, q):
        if d is None:
            return gam.at[:, strip(q), :]
        return inbound.at[wrap(me - d, owners), :, strip(q), :]

    def at(d):
        return 0 if d is None else d

    def x_copy(d, j, q, source=None):
        return pltpu.make_async_remote_copy(
            src_ref=place(d, q) if source is None else source, dst_ref=place(d, q),
            send_sem=x_s.at[at(d), j - 1], recv_sem=x_r.at[at(d), j - 1],
            device_id={"scn": group_of(wrap(chip + j, chips))}, device_id_type=MESH,
        )

    def core_copy(d, j, q, source=None):
        return pltpu.make_async_remote_copy(
            src_ref=place(d, q) if source is None else source, dst_ref=place(d, q),
            send_sem=core_s.at[at(d), j], recv_sem=core_r.at[at(d), j],
            device_id={"scn": partner}, device_id_type=MESH,
        )

    def origin(j):
        return group_of(wrap(chip - j, chips))

    def partners_origin(j):
        return wrap(chip - j, chips) * 2 + 1 - core

    def share(d, source=None):
        for j in range(1, chips):
            x_copy(d, j, mine, source).start()
        core_copy(d, 0, mine, source).start()

    def forward(d):
        for j in range(1, chips):
            x_copy(d, j, origin(j)).wait_recv()
            core_copy(d, j, origin(j)).start()

    def gathered(d):
        for j in range(chips):
            core_copy(d, j, partners_origin(j)).wait_recv()

    def drain(d):
        for j in range(1, chips):
            x_copy(d, j, mine).wait_send()
        core_copy(d, 0, mine).wait_send()
        for j in range(1, chips):
            core_copy(d, j, origin(j)).wait_send()

    share(None, gamma_hbm)
    draws_in.wait()

    def expose(blocks, h):
        flat = blocks.reshape(blocks.shape[0] * blocks.shape[1], blocks.shape[2])
        value = jnp.dot(flat, draws[...], preferred_element_type=jnp.float32).astype(jnp.bfloat16)
        shocks[pl.ds(h * per_source, per_source)] = value.reshape(per_source, blocks.shape[1], value.shape[1])

    fold[...] = jnp.zeros_like(fold)

    def step(t, carry):
        @pl.when(t < owners)
        def _():
            main_arrival(t).wait_recv()
            share(t)

        @pl.when(t == 1)
        def _():
            forward(None)

        @pl.when((t > 1) & (t <= owners))
        def _():
            forward(t - 1)

        @pl.when(t == 1)
        def _():
            for c in range(CHUNKS):
                load_copy(c).wait()

        @pl.when(t == 2)
        def _():
            expose(jnp.stack([loads[table_ref[me, k]] for k in range(per_source)]), me)

        @pl.when(t <= CHUNKS)
        def _():
            piece = delta_ref[:, pl.ds(pl.multiple_of((t - 1) * rows, rows), rows)]
            chunk = loads[pl.ds((t - 1) * some, some)].reshape(rows, depth)
            fold[...] += jnp.dot(three_parts(piece), chunk, preferred_element_type=jnp.float32)

        @pl.when(t == owners)
        def _():
            total = jnp.sum(fold[...], axis=0, keepdims=True)
            linear[...] = jnp.dot(three_parts(total), draws[...], preferred_element_type=jnp.float32)

        @pl.when(t > 2)
        def _():
            gathered(t - 2)
            h = wrap(me - (t - 2), owners)
            expose(inbound[h], h)

        return carry

    lax.fori_loop(1, owners + 2, step, 0)
    gamma_in.wait()
    gathered(None)

    columns = draws.shape[1]

    def one_slot(p, total):
        product = jnp.dot(gam[p], shocks[table_ref[owners, capacity + p]], preferred_element_type=jnp.float32)
        terms = product * shocks[table_ref[owners, p]].astype(jnp.float32)
        return total + (0.5 * table_ref[owners + 1, p].astype(jnp.float32)) * jnp.sum(terms.reshape(height // 8, 8, columns), axis=0)

    quad = lax.fori_loop(0, capacity, one_slot, jnp.zeros((8, columns), jnp.float32))
    part_sum = jnp.sum(quad, axis=0, keepdims=True) + jnp.sum(linear[...], axis=0, keepdims=True)
    sums[me] = part_sum

    def sum_copy(d):
        return pltpu.make_async_remote_copy(
            src_ref=sums.at[me], dst_ref=sums.at[me],
            send_sem=sum_s.at[d], recv_sem=sum_r.at[d],
            device_id={"fac": wrap(me + d, owners)}, device_id_type=MESH,
        )

    def sum_arrival(d):
        return pltpu.make_async_remote_copy(
            src_ref=sums.at[wrap(me - d, owners)], dst_ref=sums.at[wrap(me - d, owners)],
            send_sem=sum_s.at[d], recv_sem=sum_r.at[d],
            device_id={"fac": wrap(me + d, owners)}, device_id_type=MESH,
        )

    def start_sum(d, carry):
        sum_copy(d).start()
        return carry

    lax.fori_loop(1, owners, start_sum, 0)
    drain(None)

    def drain_step(d, carry):
        main_copy(d).wait_send()
        drain(d)
        return carry

    lax.fori_loop(1, owners, drain_step, 0)

    def wait_sum(d, carry):
        sum_arrival(d).wait_recv()
        return carry

    lax.fori_loop(1, owners, wait_sum, 0)
    result_ref[...] = jnp.sum(sums[...], axis=0)

    def drain_sum(d, carry):
        sum_copy(d).wait_send()
        return carry

    lax.fori_loop(1, owners, drain_sum, 0)


def on_device(loadings, draws, delta, gamma, pair_rows, pair_cols, pair_count):
    owners = lax.axis_size("fac")
    groups = lax.axis_size("scn")
    capacity, part, height = gamma.shape
    local_blocks = loadings.shape[0] // height
    depth, columns = draws.shape
    per_source = 2 * capacity // owners + 1
    chips = groups // 2
    smem = pl.BlockSpec(memory_space=pltpu.SMEM)
    anywhere = pl.BlockSpec(memory_space=pl.ANY)
    vmem = pl.BlockSpec(memory_space=pltpu.VMEM)
    bf16, f32, i32 = jnp.bfloat16, jnp.float32, jnp.int32
    dma = pltpu.SemaphoreType.DMA

    wanted = jnp.concatenate(
        [pair_rows.reshape(owners, capacity), pair_cols.reshape(owners, capacity)], axis=1
    )
    table = pl.pallas_call(
        functools.partial(tabulate, owners, per_source, local_blocks),
        out_shape=jax.ShapeDtypeStruct((owners + 8, 128), i32),
        in_specs=[vmem, smem],
        out_specs=vmem,
        name="tabulate",
    )(wanted, pair_count)

    result = pl.pallas_call(
        functools.partial(main_kernel, owners, groups, per_source, capacity, part),
        out_shape=jax.ShapeDtypeStruct((1, columns), f32),
        in_specs=[smem, anywhere, anywhere, vmem, anywhere],
        out_specs=vmem,
        scratch_shapes=[
            pltpu.VMEM((local_blocks, height, depth), bf16),
            pltpu.VMEM((depth, columns), bf16),
            pltpu.VMEM((local_blocks, part, depth), bf16),
            pltpu.VMEM((owners, per_source, part, depth), bf16),
            pltpu.VMEM((owners, per_source, height, depth), bf16),
            pltpu.VMEM((owners * per_source, height, columns), bf16),
            pltpu.VMEM((capacity, height, height), bf16),
            pltpu.VMEM((16, depth), f32),
            pltpu.VMEM((16, columns), f32),
            pltpu.VMEM((owners, 1, columns), f32),
            dma((CHUNKS,)),
            dma((3,)),
            dma((owners,)),
            dma((owners,)),
            dma((owners, max(chips - 1, 1))),
            dma((owners, max(chips - 1, 1))),
            dma((owners, chips)),
            dma((owners, chips)),
            dma((owners,)),
            dma((owners,)),
        ],
        compiler_params=pltpu.CompilerParams(
            collective_id=0, has_side_effects=True, vmem_limit_bytes=52 * 2**20
        ),
        name="gather_and_sum",
    )(table, loadings.reshape(local_blocks, height, depth), draws, delta.reshape(1, -1), gamma)
    return result.reshape(columns)


def solution(mesh):
    in_specs = (P("fac", None), P(None, "scn"), P("fac"), P("fac", "scn", None), P(), P(), P())
    out_specs = P("scn")
    return jax.shard_map(
        on_device, mesh=mesh, in_specs=in_specs, out_specs=out_specs, check_vma=False
    )
```

```python
import functools

import jax
import jax.numpy as jnp
from jax import lax
from jax.experimental import pallas as pl
from jax.experimental.pallas import tpu as pltpu
from jax.sharding import PartitionSpec as P

MESH = pl.DeviceIdType.MESH
CHUNKS = 8
AHEAD = 2


def tabulate(owners, per_source, local_blocks, wanted_ref, count_ref, table_ref):
    me = lax.axis_index("fac")
    wanted = wanted_ref[...]
    requests = wanted.shape[1]
    capacity = requests // 2
    f32, i32 = jnp.float32, jnp.int32
    holder = ((wanted.astype(f32) + 0.5) * (1.0 / local_blocks)).astype(i32)
    square = (requests, requests)
    earlier = (
        lax.broadcasted_iota(i32, square, 0) < lax.broadcasted_iota(i32, square, 1)
    ).astype(f32)

    def rank_of(hit):
        return jnp.dot(hit.astype(f32), earlier, preferred_element_type=f32).astype(i32)

    hit = holder == me
    rank = rank_of(hit)
    offset = wanted - me * local_blocks
    lane = lax.broadcasted_iota(i32, (owners, 128), 1)
    picks = jnp.zeros((owners, 128), i32)
    for k in range(per_source):
        pick = jnp.sum(jnp.where(hit & (rank == k), offset, 0), axis=1, keepdims=True)
        picks = picks + jnp.where(lane == k, pick, 0)
    table_ref[0:owners] = picks

    owner = lax.broadcasted_iota(i32, wanted.shape, 0)
    is_mine = owner == me
    my_wanted = jnp.sum(jnp.where(is_mine, wanted, 0), axis=0, keepdims=True)
    my_holder = jnp.sum(jnp.where(is_mine, holder, 0), axis=0, keepdims=True)
    from_holder = owner == my_holder
    position = jnp.sum(jnp.where(from_holder, rank_of(from_holder), 0), axis=0, keepdims=True)
    arrival = my_holder * per_source + position
    slot = lax.broadcasted_iota(i32, (1, capacity), 1)
    level = jnp.where(my_wanted[:, :capacity] == my_wanted[:, capacity:], 1, 2)
    level = jnp.where(slot < count_ref[me], level, 0)
    table_ref[owners:owners + 1, 0:requests] = arrival
    table_ref[owners + 1:owners + 2, 0:capacity] = level


def three_parts(values):
    first = values.astype(jnp.bfloat16).astype(jnp.float32)
    rest = values - first
    second = rest.astype(jnp.bfloat16).astype(jnp.float32)
    third = rest - second
    shape = (16, values.shape[1])
    row = lax.broadcasted_iota(jnp.int32, shape, 0)
    spread = [jnp.broadcast_to(v, shape) for v in (first, second, third)]
    zero = jnp.zeros(shape, jnp.float32)
    both = jnp.where(row == 0, spread[0], jnp.where(row == 1, spread[1], jnp.where(row == 2, spread[2], zero)))
    return both.astype(jnp.bfloat16)


def main_kernel(owners, groups, per_source, capacity, part,
                table_ref, load_hbm, draws_hbm, delta_ref, gamma_hbm,
                result_ref,
                loads, draws, strips, out_q, inbound, shocks, gam, fold, linear, sums,
                load_sem, in_sem, main_s, main_r, x_s, x_r, core_s, core_r, sum_s, sum_r):
    me = lax.axis_index("fac")
    mine = lax.axis_index("scn")
    chips = groups // 2
    core = lax.rem(mine, 2)
    chip = lax.div(mine, 2)
    partner = mine + 1 - 2 * core

    def wrap(value, size):
        return lax.rem(value + size, size)

    def peer(t):
        half, odd = lax.div(t, 2), lax.rem(t, 2)
        flips = half + odd * (owners // 2)
        other, bit = 0, 1
        while bit < owners:
            other = other + bit * lax.rem(lax.div(me, bit) + lax.div(flips, bit), 2)
            bit *= 2
        return other

    def group_of(chip_index):
        return chip_index * 2 + core

    def strip(q):
        return pl.ds(pl.multiple_of(q * part, part), part)

    barrier = pltpu.get_barrier_semaphore()
    for d in range(1, owners):
        pl.semaphore_signal(barrier, inc=1, device_id={"fac": wrap(me + d, owners)}, device_id_type=MESH)
    for j in range(1, chips):
        pl.semaphore_signal(barrier, inc=1, device_id={"scn": group_of(wrap(chip + j, chips))}, device_id_type=MESH)
    pl.semaphore_signal(barrier, inc=1, device_id={"scn": partner}, device_id_type=MESH)

    gamma_in = pltpu.make_async_copy(gamma_hbm, gam.at[:, strip(mine), :], in_sem.at[0])
    draws_in = pltpu.make_async_copy(draws_hbm, draws, in_sem.at[1])
    strips_in = pltpu.make_async_copy(load_hbm.at[:, strip(mine), :], strips, in_sem.at[2])
    strips_in.start()
    gamma_in.start()
    draws_in.start()
    local_blocks, height, depth = loads.shape
    some = local_blocks // CHUNKS
    rows = some * height

    def load_copy(c):
        return pltpu.make_async_copy(
            load_hbm.at[pl.ds(c * some, some)], loads.at[pl.ds(c * some, some)], load_sem.at[c]
        )

    for c in range(CHUNKS):
        load_copy(c).start()

    pl.semaphore_wait(barrier, owners - 1 + chips)

    def main_copy(d):
        return pltpu.make_async_remote_copy(
            src_ref=out_q.at[peer(d)], dst_ref=inbound.at[me, :, strip(mine), :],
            send_sem=main_s.at[d], recv_sem=main_r.at[d],
            device_id={"fac": peer(d)}, device_id_type=MESH,
        )

    def main_arrival(d):
        return pltpu.make_async_remote_copy(
            src_ref=out_q.at[me], dst_ref=inbound.at[peer(d), :, strip(mine), :],
            send_sem=main_s.at[d], recv_sem=main_r.at[d],
            device_id={"fac": peer(d)}, device_id_type=MESH,
        )

    strips_in.wait()

    def start_main(d, carry):
        owner = peer(d)
        for k in range(per_source):
            out_q[owner, k] = strips[table_ref[owner, k]]
        main_copy(d).start()
        return carry

    lax.fori_loop(1, 1 + min(AHEAD, owners - 1), start_main, 0)

    def place(d, q):
        if d is None:
            return gam.at[:, strip(q), :]
        return inbound.at[peer(d), :, strip(q), :]

    def at(d):
        return 0 if d is None else d

    def x_copy(d, j, q, source=None):
        return pltpu.make_async_remote_copy(
            src_ref=place(d, q) if source is None else source, dst_ref=place(d, q),
            send_sem=x_s.at[at(d), j - 1], recv_sem=x_r.at[at(d), j - 1],
            device_id={"scn": group_of(wrap(chip + j, chips))}, device_id_type=MESH,
        )

    def core_copy(d, j, q, source=None):
        return pltpu.make_async_remote_copy(
            src_ref=place(d, q) if source is None else source, dst_ref=place(d, q),
            send_sem=core_s.at[at(d), j], recv_sem=core_r.at[at(d), j],
            device_id={"scn": partner}, device_id_type=MESH,
        )

    def origin(j):
        return group_of(wrap(chip - j, chips))

    def partners_origin(j):
        return wrap(chip - j, chips) * 2 + 1 - core

    def share(d, source=None):
        for j in range(1, chips):
            x_copy(d, j, mine, source).start()
        core_copy(d, 0, mine, source).start()

    def forward(d):
        for j in range(1, chips):
            x_copy(d, j, origin(j)).wait_recv()
            core_copy(d, j, origin(j)).start()

    def gathered(d):
        for j in range(chips):
            core_copy(d, j, partners_origin(j)).wait_recv()

    def drain(d):
        for j in range(1, chips):
            x_copy(d, j, mine).wait_send()
        core_copy(d, 0, mine).wait_send()
        for j in range(1, chips):
            core_copy(d, j, origin(j)).wait_send()

    share(None, gamma_hbm)
    draws_in.wait()

    def expose(blocks, h):
        flat = blocks.reshape(blocks.shape[0] * blocks.shape[1], blocks.shape[2])
        value = jnp.dot(flat, draws[...], preferred_element_type=jnp.float32).astype(jnp.bfloat16)
        shocks[pl.ds(h * per_source, per_source)] = value.reshape(per_source, blocks.shape[1], value.shape[1])

    fold[...] = jnp.zeros_like(fold)

    def step(t, carry):
        @pl.when(t < owners)
        def _():
            main_arrival(t).wait_recv()
            share(t)

        @pl.when(t + AHEAD < owners)
        def _():
            start_main(t + AHEAD, 0)

        @pl.when(t == 1)
        def _():
            forward(None)

        @pl.when((t > 1) & (t <= owners))
        def _():
            forward(t - 1)

        @pl.when(t == 1)
        def _():
            for c in range(CHUNKS):
                load_copy(c).wait()

        @pl.when(t == 2)
        def _():
            expose(jnp.stack([loads[table_ref[me, k]] for k in range(per_source)]), me)

        @pl.when(t <= CHUNKS)
        def _():
            piece = delta_ref[:, pl.ds(pl.multiple_of((t - 1) * rows, rows), rows)]
            chunk = loads[pl.ds((t - 1) * some, some)].reshape(rows, depth)
            fold[...] += jnp.dot(three_parts(piece), chunk, preferred_element_type=jnp.float32)

        @pl.when(t == owners)
        def _():
            total = jnp.sum(fold[...], axis=0, keepdims=True)
            linear[...] = jnp.dot(three_parts(total), draws[...], preferred_element_type=jnp.float32)

        @pl.when(t > 2)
        def _():
            gathered(t - 2)
            h = peer(t - 2)
            expose(inbound[h], h)

        return carry

    lax.fori_loop(1, owners + 2, step, 0)
    gamma_in.wait()
    gathered(None)

    columns = draws.shape[1]

    def one_slot(p, total):
        product = jnp.dot(gam[p], shocks[table_ref[owners, capacity + p]], preferred_element_type=jnp.float32)
        terms = product * shocks[table_ref[owners, p]].astype(jnp.float32)
        return total + (0.5 * table_ref[owners + 1, p].astype(jnp.float32)) * jnp.sum(terms.reshape(height // 8, 8, columns), axis=0)

    quad = lax.fori_loop(0, capacity, one_slot, jnp.zeros((8, columns), jnp.float32), unroll=4)
    part_sum = jnp.sum(quad, axis=0, keepdims=True) + jnp.sum(linear[...], axis=0, keepdims=True)
    sums[me] = part_sum

    def sum_copy(d):
        return pltpu.make_async_remote_copy(
            src_ref=sums.at[me], dst_ref=sums.at[me],
            send_sem=sum_s.at[d], recv_sem=sum_r.at[d],
            device_id={"fac": peer(d)}, device_id_type=MESH,
        )

    def sum_arrival(d):
        return pltpu.make_async_remote_copy(
            src_ref=sums.at[peer(d)], dst_ref=sums.at[peer(d)],
            send_sem=sum_s.at[d], recv_sem=sum_r.at[d],
            device_id={"fac": peer(d)}, device_id_type=MESH,
        )

    def start_sum(d, carry):
        sum_copy(d).start()
        return carry

    lax.fori_loop(1, owners, start_sum, 0)
    drain(None)

    def drain_step(d, carry):
        main_copy(d).wait_send()
        drain(d)
        return carry

    lax.fori_loop(1, owners, drain_step, 0)

    def wait_sum(d, carry):
        sum_arrival(d).wait_recv()
        return carry

    lax.fori_loop(1, owners, wait_sum, 0)
    result_ref[...] = jnp.sum(sums[...], axis=0)

    def drain_sum(d, carry):
        sum_copy(d).wait_send()
        return carry

    lax.fori_loop(1, owners, drain_sum, 0)


def on_device(loadings, draws, delta, gamma, pair_rows, pair_cols, pair_count):
    owners = lax.axis_size("fac")
    groups = lax.axis_size("scn")
    capacity, part, height = gamma.shape
    local_blocks = loadings.shape[0] // height
    depth, columns = draws.shape
    per_source = 2 * capacity // owners + 1
    chips = groups // 2
    smem = pl.BlockSpec(memory_space=pltpu.SMEM)
    anywhere = pl.BlockSpec(memory_space=pl.ANY)
    vmem = pl.BlockSpec(memory_space=pltpu.VMEM)
    bf16, f32, i32 = jnp.bfloat16, jnp.float32, jnp.int32
    dma = pltpu.SemaphoreType.DMA

    wanted = jnp.concatenate(
        [pair_rows.reshape(owners, capacity), pair_cols.reshape(owners, capacity)], axis=1
    )
    table = pl.pallas_call(
        functools.partial(tabulate, owners, per_source, local_blocks),
        out_shape=jax.ShapeDtypeStruct((owners + 8, 128), i32),
        in_specs=[vmem, smem],
        out_specs=vmem,
        name="tabulate",
    )(wanted, pair_count)

    result = pl.pallas_call(
        functools.partial(main_kernel, owners, groups, per_source, capacity, part),
        out_shape=jax.ShapeDtypeStruct((1, columns), f32),
        in_specs=[smem, anywhere, anywhere, vmem, anywhere],
        out_specs=vmem,
        scratch_shapes=[
            pltpu.VMEM((local_blocks, height, depth), bf16),
            pltpu.VMEM((depth, columns), bf16),
            pltpu.VMEM((local_blocks, part, depth), bf16),
            pltpu.VMEM((owners, per_source, part, depth), bf16),
            pltpu.VMEM((owners, per_source, height, depth), bf16),
            pltpu.VMEM((owners * per_source, height, columns), bf16),
            pltpu.VMEM((capacity, height, height), bf16),
            pltpu.VMEM((16, depth), f32),
            pltpu.VMEM((16, columns), f32),
            pltpu.VMEM((owners, 1, columns), f32),
            dma((CHUNKS,)),
            dma((3,)),
            dma((owners,)),
            dma((owners,)),
            dma((owners, max(chips - 1, 1))),
            dma((owners, max(chips - 1, 1))),
            dma((owners, chips)),
            dma((owners, chips)),
            dma((owners,)),
            dma((owners,)),
        ],
        compiler_params=pltpu.CompilerParams(
            collective_id=0, has_side_effects=True, vmem_limit_bytes=63 * 2**20
        ),
        name="gather_and_sum",
    )(table, loadings.reshape(local_blocks, height, depth), draws, delta.reshape(1, -1), gamma)
    return result.reshape(columns)


def solution(mesh):
    in_specs = (P("fac", None), P(None, "scn"), P("fac"), P("fac", "scn", None), P(), P(), P())
    out_specs = P("scn")
    return jax.shard_map(
        on_device, mesh=mesh, in_specs=in_specs, out_specs=out_specs, check_vma=False
    )
```
